256 devices in a mesh: ctx: 16 (over x_lo, y, core), tp: 16 (over x_hi, z).
Axes of the slice: x: 4 (x_hi: 2, x_lo: 2; x = x_hi * 2 + x_lo), y: 4, z: 8, core: 2. Of those that a mesh axis runs over, the one named last changes fastest.
Arguments:
- features: bfloat16 [4096, 3, 8192], P('ctx', None, 'tp'), may hold values from -6 to 6
- short_filter: float32 [3, 7, 8192], P(None, None, 'tp'), may hold values from -2 to 2
- decay_rate: float32 [16, 8192], P(None, 'tp'), may hold values from 0.05 to 136.533333
- residue: float32 [16, 8192], P(None, 'tp'), may hold values from -1.5 to 1.5
- out_weight: bfloat16 [8192, 8192], P('tp'), may hold values from -0.0625 to 0.0625
Outputs:
- block_output: bfloat16 [4096, 8192], P(('ctx', 'tp'))
The draws below stay inside these ranges and needn't reach their ends.
All inputs are finite; a program needn't handle non-finite values.
Results may differ from the reference program's by a relative error of at most 0.027.
Values may be sent and summed in bfloat16 or wider, within the bound.
No kernel may reach another device: no remote copies, remote signals or barrier semaphores. Data moves between devices by JAX's collectives and lax.ppermute only.
A program may use at most 64 MiB of HBM per device.

```python
import jax
import jax.numpy as jnp
from jax import lax

D = 8192
MODES = 16
TAPS = 7
TOKENS = 4096
N_TP = 16


def draw_decay_rate(key, part):
    key = jax.random.fold_in(key, 11)
    key_pick, key_base = jax.random.split(key, 2)
    pick = jax.random.uniform(key_pick, (MODES, D), jnp.float32)
    base = jax.random.uniform(key_base, (MODES, D), jnp.float32)
    slow_share = 0.4
    fast_share = 0.3
    slow_rate = 0.05 * 40.0 ** base
    middle_rate = 2.0 * (TOKENS / 100.0) ** base
    fast_rate = TOKENS / 50.0 * (5.0 / 3.0) ** base
    chosen = jnp.where(pick < slow_share, slow_rate, jnp.where(pick < slow_share + fast_share, fast_rate, middle_rate))
    return chosen.astype(jnp.float32)


def shard_levels(own_key, dims, cuts, low, largest):
    factor_of, own = 1.0, jax.random.fold_in(own_key, 6)
    for position, shards_of in cuts:
        heights = jnp.exp(jax.random.uniform(jax.random.fold_in(own, position), (shards_of,), jnp.float32, low / len(cuts), largest / len(cuts)))
        factor_of = factor_of * jnp.repeat(heights, dims[position] // shards_of).reshape([-1 if axis == position else 1 for axis in range(len(dims))])
    return factor_of


def centred(key, extent, scale, limit, pieces=(), kind=jnp.bfloat16):
    entries = scale * jax.random.normal(key, extent, jnp.float32)
    if pieces:
        entries = entries * shard_levels(key, extent, pieces, -0.22, 0.18)
    return jnp.clip(entries, -limit, limit).astype(kind)


def setup_inputs(seed: int = 0) -> dict:
    key_list = jax.random.split(jax.random.key(seed), 6)
    return {
        "features": centred(key_list[0], (TOKENS, 3, D), 1.0, 6.0, ((0, 16), (2, 16))),
        "short_filter": centred(key_list[1], (3, TAPS, D), TAPS ** -0.5, 2.0, ((2, 16),), jnp.float32),
        "decay_rate": draw_decay_rate(jax.random.fold_in(key_list[5], 71), 0),
        "residue": centred(key_list[3], (MODES, D), 0.25, 1.5, ((1, 16),), jnp.float32),
        "out_weight": centred(key_list[4], (D, D), D ** -0.5, 0.0625, ((0, 16),)),
    }


def chan_output(features, short_filter, decay_rate, residue, out_weight, first, span):
    chan_block = lax.dynamic_slice_in_dim(features, first, span, 2).astype(jnp.float32)
    tap_block = lax.dynamic_slice_in_dim(short_filter, first, span, 2)
    padded = jnp.pad(chan_block, ((TAPS - 1, 0), (0, 0), (0, 0)))
    featured = tap_block[:, 0, :] * padded[TAPS - 1:TAPS - 1 + TOKENS]
    for j in range(1, TAPS):
        featured = featured + tap_block[:, j, :] * padded[TAPS - 1 - j:TAPS - 1 - j + TOKENS]
    queries = featured[:, 0]
    signal = featured[:, 1] * featured[:, 2]
    rates = lax.dynamic_slice_in_dim(decay_rate, first, span, 1)
    mode_res = lax.dynamic_slice_in_dim(residue, first, span, 1)
    mode_gain = jnp.sqrt(1.0 / TOKENS - jnp.expm1(-2.0 * rates / TOKENS))
    mode_coef = mode_res * mode_gain
    positions = jnp.arange(TOKENS).astype(jnp.float32)[:, None] / TOKENS
    kernel = jnp.zeros((TOKENS, span), jnp.float32)
    for m in range(MODES):
        kernel = kernel + mode_coef[m] * jnp.exp(-positions * rates[m])
    length = 2 * TOKENS
    spectrum = jnp.fft.rfft(signal, length, axis=0) * jnp.fft.rfft(kernel, length, axis=0)
    convolved = jnp.fft.irfft(spectrum, length, axis=0)[:TOKENS]
    gated = (queries * convolved).astype(jnp.bfloat16)
    weight_rows = lax.dynamic_slice_in_dim(out_weight, first, span, 0)
    return jnp.dot(gated, weight_rows, preferred_element_type=jnp.float32)

def reference(features, short_filter, decay_rate, residue, out_weight):
    span = D // N_TP

    def accumulate(index, total):
        group_term = chan_output(features, short_filter, decay_rate, residue, out_weight, index * span, span)
        rounded = lax.optimization_barrier(group_term.astype(jnp.bfloat16))
        return total + rounded.astype(jnp.float32)
    total = lax.fori_loop(0, N_TP, accumulate, jnp.zeros((TOKENS, D), jnp.float32))
    return total.astype(jnp.bfloat16)
```

```python
import functools

import jax
import jax.numpy as jnp
from jax import lax
from jax.experimental import pallas as pl
from jax.experimental.pallas import tpu as pltpu
from jax.sharding import PartitionSpec as P

TAPS = 7
MODES = 16
SUB = 8
LANES = 128
NZ = 8
N_CTX = 16
HALO = 16

f32 = jnp.float32
bf16 = jnp.bfloat16


def signal_kernel(ctx_ref, x_ref, halo_ref, taps_ref, a_ref, sig_ref, q_ref, ends_ref, send_ref, pad, ends, step_powers):
    rows = x_ref.shape[1]
    run = rows // SUB
    for b in range(3):
        pad[b, :HALO] = halo_ref[b].astype(f32)
        pad[b, HALO:] = x_ref[b].astype(f32)
    wide = (SUB, LANES)
    for b in range(3):
        taps = [jnp.broadcast_to(taps_ref[b, j : j + 1, :], wide) for j in range(TAPS)]
        window = [pad[b, pl.ds(HALO - j, SUB, stride=run), :] for j in range(1, TAPS)]
        for t in range(run):
            window = [pad[b, pl.ds(HALO + t, SUB, stride=run), :]] + window
            total = taps[0] * window[0]
            for j in range(1, TAPS):
                total = total + taps[j] * window[j]
            if b == 0:
                q_ref[t] = total
            elif b == 1:
                sig_ref[t] = total
            else:
                sig_ref[t] = sig_ref[t] * total
            window = window[: TAPS - 1]
    for first in range(0, MODES, 8):
        decay = [jnp.broadcast_to(a_ref[m : m + 1, :], wide) for m in range(first, first + 8)]
        state = [sig_ref[0]] * 8
        for t in range(1, run):
            now = sig_ref[t]
            state = [d * s + now for d, s in zip(decay, state)]
        for m in range(8):
            ends[first + m] = state[m]
            ends_ref[first + m] = state[m]
    a = a_ref[...]
    power = a
    for _ in range(run.bit_length() - 1):
        power = power * power
    total = ends[:, 0, :]
    for j in range(1, SUB):
        total = power * total + ends[:, j, :]
    whole = power
    for _ in range(SUB.bit_length() - 1):
        whole = whole * whole
    me = ctx_ref[0]
    for d in range(N_CTX):
        step_powers[d] = total
        total = total * whole
    for d in range(N_CTX):
        away = jnp.maximum(d - me - 1, 0)
        sent = step_powers[away]
        send_ref[d] = jnp.where(d > me, sent, 0.0).astype(bf16)


def gate_kernel(pos_ref, sig_ref, q_ref, ends_ref, a_ref, coef_ref, recv_ref, out_ref, starts, conv, gated):
    run = sig_ref.shape[0]
    wide = (SUB, LANES)
    a = a_ref[...]
    power = a
    for _ in range(run.bit_length() - 1):
        power = power * power
    state = recv_ref[0].astype(f32)
    for p in range(1, N_CTX):
        state = state + recv_ref[p].astype(f32)
    for j in range(SUB):
        starts[:, j, :] = state
        if j < SUB - 1:
            state = power * state + ends_ref[:, j, :]
    for first in range(0, MODES, 8):
        decay = [jnp.broadcast_to(a_ref[m : m + 1, :], wide) for m in range(first, first + 8)]
        coef = [jnp.broadcast_to(coef_ref[m : m + 1, :], wide) for m in range(first, first + 8)]
        state = [starts[m] for m in range(first, first + 8)]
        for t in range(run):
            now = sig_ref[t]
            state = [d * s + now for d, s in zip(decay, state)]
            terms = [c * s for c, s in zip(coef, state)]
            while len(terms) > 1:
                terms = [terms[i] + terms[i + 1] for i in range(0, len(terms), 2)]
            if first == 0:
                conv[t] = terms[0]
            else:
                gated[pl.ds(t, SUB, stride=run), :] = (conv[t] + terms[0]) * q_ref[t]
    half, z = pos_ref[0], pos_ref[1]
    for h in range(2):
        for k in range(NZ):
            block = lax.rem(half + h, 2) * NZ + lax.rem(z + k, NZ)
            rows = gated[pl.ds(pl.multiple_of(block * 16, 16), 16), :]
            out_ref[(h * NZ + k) * 16 : (h * NZ + k + 1) * 16, :] = rows.astype(bf16)


def z_pairs(by):
    return [(h * NZ + z, h * NZ + (z + by) % NZ) for h in range(2) for z in range(NZ)]


def half_pairs():
    return [(i, (i + NZ) % (2 * NZ)) for i in range(2 * NZ)]


def ring(blocks, more_left):
    rights, lefts = (NZ // 2 - 1, NZ // 2) if more_left else (NZ // 2, NZ // 2 - 1)
    right = blocks[rights]
    left = blocks[-lefts % NZ]
    for s in range(NZ // 2):
        if s < rights:
            right = lax.ppermute(right, "tp", z_pairs(1))
        if s < lefts:
            left = lax.ppermute(left, "tp", z_pairs(-1))
        if s < rights - 1:
            right = (right.astype(f32) + blocks[rights - 1 - s].astype(f32)).astype(bf16)
        if s < lefts - 1:
            left = (left.astype(f32) + blocks[-(lefts - 1 - s) % NZ].astype(f32)).astype(bf16)
    return right.astype(f32) + left.astype(f32) + blocks[0].astype(f32)


def reduce_columns(gated, weight, more_left):
    part = jnp.dot(gated, weight, preferred_element_type=f32).astype(bf16)
    part = part.reshape(2, NZ, 16, -1)
    both = ring([part[:, k] for k in range(NZ)], more_left)
    other = lax.ppermute(both[1].astype(bf16), "tp", half_pairs())
    return (both[0] + other.astype(f32)).astype(bf16)


def local(features, short_filter, decay_rate, residue, out_weight):
    rows, _, chans = features.shape
    n_ctx = lax.axis_size("ctx")
    inv_tokens = 1.0 / (rows * n_ctx)
    run = rows // SUB
    ctx = lax.axis_index("ctx")
    tp = lax.axis_index("tp")
    halo = lax.ppermute(features[rows - HALO :], "ctx", [(i, i + 1) for i in range(n_ctx - 1)])
    halo = jnp.transpose(halo, (1, 0, 2))
    x = jnp.transpose(features, (1, 0, 2))
    a = jnp.exp(-decay_rate * inv_tokens)
    coef = residue * jnp.sqrt(inv_tokens - jnp.expm1(-2.0 * decay_rate * inv_tokens))
    groups = chans // LANES

    def lanes(*lead):
        return pl.BlockSpec((*lead, LANES), lambda g, *_: (0,) * len(lead) + (g,))

    sig, q, ends, send = pl.pallas_call(
        signal_kernel,
        grid_spec=pltpu.PrefetchScalarGridSpec(
            num_scalar_prefetch=1,
            grid=(groups,),
            in_specs=[lanes(3, rows), lanes(3, HALO), lanes(3, TAPS), lanes(MODES)],
            out_specs=[lanes(run, SUB), lanes(run, SUB), lanes(MODES, SUB), lanes(n_ctx, MODES)],
            scratch_shapes=[
                pltpu.VMEM((3, HALO + rows, LANES), f32),
                pltpu.VMEM((MODES, SUB, LANES), f32),
                pltpu.VMEM((N_CTX, MODES, LANES), f32),
            ],
        ),
        out_shape=[
            jax.ShapeDtypeStruct((run, SUB, chans), f32),
            jax.ShapeDtypeStruct((run, SUB, chans), f32),
            jax.ShapeDtypeStruct((MODES, SUB, chans), f32),
            jax.ShapeDtypeStruct((n_ctx, MODES, chans), bf16),
        ],
        name="signal",
    )(jnp.full((1,), ctx, jnp.int32), x, halo, short_filter, a)
    recv = lax.all_to_all(send, "ctx", 0, 0, tiled=True)
    gated = pl.pallas_call(
        gate_kernel,
        grid_spec=pltpu.PrefetchScalarGridSpec(
            num_scalar_prefetch=1,
            grid=(groups,),
            in_specs=[
                lanes(run, SUB),
                lanes(run, SUB),
                lanes(MODES, SUB),
                lanes(MODES),
                lanes(MODES),
                lanes(n_ctx, MODES),
            ],
            out_specs=lanes(rows),
            scratch_shapes=[
                pltpu.VMEM((MODES, SUB, LANES), f32),
                pltpu.VMEM((run, SUB, LANES), f32),
                pltpu.VMEM((rows, LANES), f32),
            ],
        ),
        out_shape=jax.ShapeDtypeStruct((rows, chans), bf16),
        name="gate",
    )(jnp.stack([tp // NZ, tp % NZ]).astype(jnp.int32), sig, q, ends, a, coef, recv)
    cols = out_weight.shape[1] // 2
    out = [reduce_columns(gated, out_weight[:, i * cols : (i + 1) * cols], i == 1) for i in range(2)]
    return jnp.concatenate(out, axis=1)


def solution(mesh):
    in_specs = (
        P("ctx", None, "tp"),
        P(None, None, "tp"),
        P(None, "tp"),
        P(None, "tp"),
        P("tp", None),
    )
    out_specs = P(("ctx", "tp"), None)
    return jax.shard_map(local, mesh=mesh, in_specs=in_specs, out_specs=out_specs, check_vma=False)
```

```python
import functools

import jax
import jax.numpy as jnp
from jax import lax
from jax.experimental import pallas as pl
from jax.experimental.pallas import tpu as pltpu
from jax.sharding import PartitionSpec as P

TAPS = 7
MODES = 16
SUB = 8
LANES = 128
NZ = 8
HALO = 16
BACK = TAPS - 1

f32 = jnp.float32
bf16 = jnp.bfloat16
VMEM = pltpu.VMEM


def one_hot(rows, cols, pick):
    row = lax.broadcasted_iota(jnp.int32, (rows, LANES), 0)
    want = pick(row)
    col = lax.broadcasted_iota(jnp.int32, (rows, LANES), 1)
    tiles = [jnp.where(want == col + c, 1.0, 0.0).astype(bf16) for c in range(0, cols, LANES)]
    return jnp.concatenate(tiles, axis=1)


def spread_matrix(rows):
    run = rows // SUB
    return one_hot((run + BACK) * SUB, rows, lambda r: run * (r % SUB) + r // SUB - BACK)


def edge_rows(halo_ref, branch):
    first = one_hot(BACK * SUB, LANES, lambda r: jnp.where(r % SUB == 0, r // SUB + HALO - BACK, -1))[:, :HALO]
    return jnp.dot(first, halo_ref[branch], preferred_element_type=f32)


def fir(taps_ref, branch, read, lanes, times, emit):
    taps = [jnp.broadcast_to(taps_ref[branch, j : j + 1, lanes], (SUB, LANES)) for j in range(TAPS)]
    window = [read(times[0] + e) for e in range(BACK)][::-1]
    for t in times:
        window = [read(t + BACK)] + window
        terms = [taps[j] * window[j] for j in range(TAPS)]
        while len(terms) > 1:
            terms = [terms[i] + terms[i + 1] for i in range(0, len(terms) - 1, 2)] + terms[len(terms) // 2 * 2 :]
        emit(t, terms[0])
        window = window[:BACK]


def at(t):
    return slice(t * SUB, (t + 1) * SUB)


def lane_loop(chans, group):
    def step(g, _):
        group(pl.ds(pl.multiple_of(g * LANES, LANES), LANES))
        return 0

    lax.fori_loop(0, chans // LANES, step, 0)


def wide_rows(ref, lanes, modes):
    return [jnp.broadcast_to(ref[m : m + 1, lanes], (SUB, LANES)) for m in modes]


def run_states(decay, state, read, times):
    for t in times:
        now = read(t)
        state = [now] * len(decay) if state is None else [d * s + now for d, s in zip(decay, state)]
    return state


def bulk_kernel(
    tokens, x_hbm, taps_hbm, rate_hbm, zero_ref, head_ref, sig_ref, late_ref, taps_ref, rate_ref, x_ref, px_ref, sems
):
    rows = x_ref.shape[1]
    run = rows // SUB
    copies = {b: pltpu.make_async_copy(x_hbm.at[b], x_ref.at[b], sems.at[b]) for b in (1, 2, 0)}
    small = [
        pltpu.make_async_copy(taps_hbm, taps_ref, sems.at[3]),
        pltpu.make_async_copy(rate_hbm, rate_ref, sems.at[4]),
    ]
    for c in [*copies.values(), *small]:
        c.start()
    move = spread_matrix(rows)
    for b, c in copies.items():
        c.wait()
        moved = jnp.dot(move, x_ref[b], preferred_element_type=f32)
        if b == 0:
            zero_ref[...] = moved
        else:
            px_ref[b - 1] = moved
            head_ref[b - 1] = moved[: 2 * BACK * SUB]
    for c in small:
        c.wait()

    def group(lanes):
        def put(t, v):
            sig_ref[at(t), lanes] = v

        def mul(t, v):
            sig_ref[at(t), lanes] = sig_ref[at(t), lanes] * v

        late = range(BACK, run)
        fir(taps_ref, 1, lambda e: px_ref[0, at(e), lanes], lanes, late, put)
        fir(taps_ref, 2, lambda e: px_ref[1, at(e), lanes], lanes, late, mul)
        decay = [jnp.exp(r * (-1.0 / tokens)) for r in wide_rows(rate_ref, lanes, range(MODES))]
        state = run_states(decay, None, lambda t: sig_ref[at(t), lanes], late)
        for m in range(MODES):
            late_ref[m, :, lanes] = state[m]

    lane_loop(x_ref.shape[2], group)


def edge_kernel(
    rows, tokens, head_ref, halo_ref, taps_ref, rate_ref, late_ref, early_ref, ends_ref, send_ref, edges, faded
):
    run = rows // SUB
    n_ctx = send_ref.shape[0]
    for b in (1, 2):
        edges[b - 1] = head_ref[b - 1, : BACK * SUB] + edge_rows(halo_ref, b)
    me = lax.axis_index("ctx")
    below = (SUB - 1 - lax.broadcasted_iota(jnp.int32, (SUB, LANES), 0)).astype(f32) * (-run / tokens)

    def group(lanes):
        def put(t, v):
            early_ref[at(t), lanes] = v

        def mul(t, v):
            early_ref[at(t), lanes] = early_ref[at(t), lanes] * v

        for b, emit in ((1, put), (2, mul)):
            fir(
                taps_ref,
                b,
                lambda e, b=b: edges[b - 1, at(e), lanes] if e < BACK else head_ref[b - 1, at(e), lanes],
                lanes,
                range(BACK),
                emit,
            )
        rate = wide_rows(rate_ref, lanes, range(MODES))
        decay = [jnp.exp(r * (-1.0 / tokens)) for r in rate]
        state = run_states(decay, None, lambda t: early_ref[at(t), lanes], range(BACK))
        for m in range(MODES):
            end = late_ref[m, :, lanes] + state[m] * jnp.exp(rate[m] * (-(run - BACK) / tokens))
            ends_ref[m, :, lanes] = end
            faded[m] = end * jnp.exp(rate[m] * below)
        total = jnp.sum(faded[...], axis=1)
        whole = jnp.exp(rate_ref[:, lanes] * (-rows / tokens))
        for d in range(n_ctx):
            send_ref[d, :, lanes] = jnp.where(d > me, total, 0.0).astype(bf16)
            total = jnp.where(d > me, total * whole, total)

    lane_loop(head_ref.shape[2], group)


def inner_kernel(
    tokens,
    px_ref,
    halo_ref,
    taps_ref,
    rate_ref,
    coef_ref,
    sig_ref,
    early_ref,
    ends_ref,
    q_ref,
    y_ref,
    lead_ref,
    turn_ref,
    edges,
):
    rows = q_ref.shape[0]
    run = rows // SUB
    edges[...] = px_ref[: BACK * SUB] + edge_rows(halo_ref, 0)
    sub = lax.broadcasted_iota(jnp.int32, (SUB, LANES), 0)
    sub_time = (sub * run + 1).astype(f32) * (-1.0 / tokens)

    def group(lanes):
        def put(t, v):
            q_ref[at(t), lanes] = v

        def signal(t):
            return early_ref[at(t), lanes] if t < BACK else sig_ref[at(t), lanes]

        fir(
            taps_ref,
            0,
            lambda e: edges[at(e), lanes] if e < BACK else px_ref[at(e), lanes],
            lanes,
            range(run),
            put,
        )
        for first in range(0, MODES, 8):
            modes = range(first, first + 8)
            coef = wide_rows(coef_ref, lanes, modes)
            rate = wide_rows(rate_ref, lanes, modes)
            decay = [jnp.exp(r * (-1.0 / tokens)) for r in rate]
            state = []
            for i, m in enumerate(modes):
                lead_ref[m, :, lanes] = coef[i] * jnp.exp(rate[i] * sub_time)
                s = ends_ref[m, :, lanes]
                for by in (1, 2, 4):
                    moved = jnp.where(sub >= by, pltpu.roll(s, by, 0), 0.0)
                    s = s + moved * jnp.exp(rate[i] * (-by * run / tokens))
                state.append(jnp.where(sub >= 1, pltpu.roll(s, 1, 0), 0.0))
            for t in range(run):
                state = run_states(decay, state, signal, [t])
                terms = [c * s for c, s in zip(coef, state)]
                while len(terms) > 1:
                    terms = [terms[i] + terms[i + 1] for i in range(0, len(terms), 2)]
                y_ref[at(t), lanes] = terms[0] if first == 0 else y_ref[at(t), lanes] + terms[0]

    lane_loop(q_ref.shape[1], group)
    tp = lax.axis_index("tp")
    half, z = tp // NZ, tp % NZ

    def natural(o):
        block = ((half + o // (NZ * 16)) % 2) * NZ + (z + o // 16) % NZ
        n = block * 16 + o % 16
        return (n % run) * SUB + n // run

    turn_ref[...] = one_hot(rows, rows, natural)


def column_copies(weight_hbm, weight, sems, base):
    tiles = sems.shape[0]
    tile = weight.shape[1] // tiles
    copies = []
    for i in range(tiles):
        here = slice(i * tile, (i + 1) * tile)
        there = slice(base + i * tile, base + (i + 1) * tile)
        copies.append((here, pltpu.make_async_copy(weight_hbm.at[:, there], weight.at[:, here], sems.at[i])))
    for _, copy in copies:
        copy.start()
    return copies


def times(left, copies, weight, out_ref):
    for here, copy in copies:
        copy.wait()
        out_ref[:, here] = jnp.dot(left, weight[:, here], preferred_element_type=f32).astype(bf16)


def gate_kernel(
    tokens, weight_hbm, recv_ref, rate_ref, lead_ref, y_ref, q_ref, turn_ref, gated_ref, part_ref, flat, weight, sems
):
    copies = column_copies(weight_hbm, weight, sems, 0)
    n_ctx = recv_ref.shape[0]
    run = y_ref.shape[0] // SUB

    def group(lanes):
        start = recv_ref[0, :, lanes].astype(f32)
        for p in range(1, n_ctx):
            start = start + recv_ref[p, :, lanes].astype(f32)
        state = [jnp.broadcast_to(start[m : m + 1], (SUB, LANES)) * lead_ref[m, :, lanes] for m in range(MODES)]
        decay = [jnp.exp(r * (-1.0 / tokens)) for r in wide_rows(rate_ref, lanes, range(MODES))]
        for t in range(run):
            terms = [y_ref[at(t), lanes]] + state
            while len(terms) > 1:
                terms = [terms[i] + terms[i + 1] for i in range(0, len(terms) - 1, 2)] + terms[len(terms) // 2 * 2 :]
            flat[at(t), lanes] = terms[0] * q_ref[at(t), lanes]
            if t < run - 1:
                state = [d * s for d, s in zip(decay, state)]

    lane_loop(y_ref.shape[1], group)
    gated = jnp.dot(turn_ref[...], flat[...].astype(bf16), preferred_element_type=f32).astype(bf16)
    gated_ref[...] = gated
    times(gated, copies, weight, part_ref)


def project_kernel(base, weight_hbm, gated_ref, part_ref, weight, sems):
    copies = column_copies(weight_hbm, weight, sems, base)
    times(gated_ref[...], copies, weight, part_ref)


def z_pairs(by):
    return [(h * NZ + z, h * NZ + (z + by) % NZ) for h in range(2) for z in range(NZ)]


def half_pairs():
    return [(i, (i + NZ) % (2 * NZ)) for i in range(2 * NZ)]


def ring(blocks, more_left):
    rights, lefts = (NZ // 2 - 1, NZ // 2) if more_left else (NZ // 2, NZ // 2 - 1)
    right = blocks[rights]
    left = blocks[-lefts % NZ]
    for s in range(NZ // 2):
        if s < rights:
            right = lax.ppermute(right, "tp", z_pairs(1))
        if s < lefts:
            left = lax.ppermute(left, "tp", z_pairs(-1))
        if s < rights - 1:
            right = (right.astype(f32) + blocks[rights - 1 - s].astype(f32)).astype(bf16)
        if s < lefts - 1:
            left = (left.astype(f32) + blocks[-(lefts - 1 - s) % NZ].astype(f32)).astype(bf16)
    return right.astype(f32) + left.astype(f32) + blocks[0].astype(f32)


def reduce_columns(part, more_left):
    part = part.reshape(2, NZ, 16, -1)
    both = ring([part[:, k] for k in range(NZ)], more_left)
    other = lax.ppermute(both[1].astype(bf16), "tp", half_pairs())
    return (both[0] + other.astype(f32)).astype(bf16)


def call(kernel, outs, scratch, name, flops, *args, far=()):
    in_specs = [pl.BlockSpec(memory_space=pl.ANY)] * len(far) + [pl.BlockSpec(memory_space=VMEM)] * len(args)
    args = [pltpu.with_memory_space_constraint(x, pltpu.HBM) for x in far] + [
        pltpu.with_memory_space_constraint(x, VMEM) for x in args
    ]
    return pl.pallas_call(
        kernel,
        in_specs=in_specs,
        out_specs=[pl.BlockSpec(memory_space=VMEM)] * len(outs),
        out_shape=[VMEM(s, d) for s, d in outs],
        scratch_shapes=[s if not isinstance(s, tuple) else VMEM(*s) for s in scratch],
        compiler_params=pltpu.CompilerParams(vmem_limit_bytes=16 * 2**20),
        cost_estimate=pl.CostEstimate(flops=flops, bytes_accessed=4 * 2**20, transcendentals=0),
        name=name,
    )(*args)


def local(features, short_filter, decay_rate, residue, out_weight):
    rows, branches, chans = features.shape
    n_ctx = lax.axis_size("ctx")
    tokens = rows * n_ctx
    run = rows // SUB
    halo = lax.ppermute(features[rows - HALO :], "ctx", [(i, i + 1) for i in range(n_ctx - 1)])
    halo = jnp.transpose(halo, (1, 0, 2))
    x = jnp.transpose(features, (1, 0, 2))
    wide = ((rows, chans), f32)
    states = ((MODES, SUB, chans), f32)
    moved = ((run + BACK) * SUB, chans)
    head = 2 * BACK * SUB
    zero, heads, sig, late, taps, rate = call(
        functools.partial(bulk_kernel, tokens),
        [(moved, f32), ((2, head, chans), f32), wide, states, (short_filter.shape, f32), (decay_rate.shape, f32)],
        [((branches, rows, chans), bf16), ((2, *moved), f32), pltpu.SemaphoreType.DMA((5,))],
        "bulk",
        4 * rows * chans * MODES,
        far=(x, short_filter, decay_rate),
    )
    early, ends, send = call(
        functools.partial(edge_kernel, rows, tokens),
        [((BACK * SUB, chans), f32), states, ((n_ctx, MODES, chans), bf16)],
        [((2, BACK * SUB, chans), f32), ((MODES, SUB, LANES), f32)],
        "edge",
        rows * chans * MODES,
        heads,
        halo,
        taps,
        rate,
        late,
    )
    recv = lax.all_to_all(send, "ctx", 0, 0, tiled=True)
    late_rate, late_residue, _ = lax.optimization_barrier((decay_rate, residue, early))
    coef = late_residue * jnp.sqrt(1.0 / tokens - jnp.expm1(late_rate * (-2.0 / tokens)))
    q, y, lead, turn = call(
        functools.partial(inner_kernel, tokens),
        [wide, wide, states, ((rows, rows), bf16)],
        [((BACK * SUB, chans), f32)],
        "inner",
        8 * rows * chans * MODES,
        zero,
        halo,
        taps,
        rate,
        coef,
        sig,
        early,
        ends,
    )
    cols = out_weight.shape[1] // 2
    stream = [((chans, cols), bf16), pltpu.SemaphoreType.DMA((8,))]
    gated, first = call(
        functools.partial(gate_kernel, tokens),
        [((rows, chans), bf16), ((rows, cols), bf16)],
        [wide, *stream],
        "gate",
        2 * rows * chans * cols,
        recv,
        rate,
        lead,
        y,
        q,
        turn,
        far=(out_weight,),
    )
    (second,) = call(
        functools.partial(project_kernel, cols),
        [((rows, cols), bf16)],
        stream,
        "project",
        2 * rows * chans * cols,
        gated,
        far=(out_weight,),
    )
    out = [reduce_columns(first, False), reduce_columns(second, True)]
    return jnp.concatenate(out, axis=1)


def solution(mesh):
    in_specs = (
        P("ctx", None, "tp"),
        P(None, None, "tp"),
        P(None, "tp"),
        P(None, "tp"),
        P("tp", None),
    )
    out_specs = P(("ctx", "tp"), None)
    return jax.shard_map(local, mesh=mesh, in_specs=in_specs, out_specs=out_specs, check_vma=False)
```

```python
import functools

import jax
import jax.numpy as jnp
from jax import lax
from jax.experimental import pallas as pl
from jax.experimental.pallas import tpu as pltpu
from jax.sharding import PartitionSpec as P

TAPS = 7
MODES = 16
SUB = 8
LANES = 128
NZ = 8
HALO = 16
READY = 1024
MEET = (2, 0)
WIDTHS = (4096, 4096)
BACK = TAPS - 1

f32 = jnp.float32
bf16 = jnp.bfloat16
VMEM = pltpu.VMEM


def one_hot(rows, cols, pick):
    row = lax.broadcasted_iota(jnp.int32, (rows, LANES), 0)
    want = pick(row)
    col = lax.broadcasted_iota(jnp.int32, (rows, LANES), 1)
    tiles = [jnp.where(want == col + c, 1.0, 0.0).astype(bf16) for c in range(0, cols, LANES)]
    return jnp.concatenate(tiles, axis=1)


def spread_matrix(rows):
    run = rows // SUB
    return one_hot((run + BACK) * SUB, rows, lambda r: run * (r % SUB) + r // SUB - BACK)


def edge_rows(halo_ref, branch):
    first = one_hot(BACK * SUB, LANES, lambda r: jnp.where(r % SUB == 0, r // SUB + HALO - BACK, -1))[:, :HALO]
    return jnp.dot(first, halo_ref[branch], preferred_element_type=f32)


def fir(taps_ref, branch, read, lanes, times, emit):
    taps = [jnp.broadcast_to(taps_ref[branch, j : j + 1, lanes], (SUB, LANES)) for j in range(TAPS)]
    window = [read(times[0] + e) for e in range(BACK)][::-1]
    for t in times:
        window = [read(t + BACK)] + window
        terms = [taps[j] * window[j] for j in range(TAPS)]
        while len(terms) > 1:
            terms = [terms[i] + terms[i + 1] for i in range(0, len(terms) - 1, 2)] + terms[len(terms) // 2 * 2 :]
        emit(t, terms[0])
        window = window[:BACK]


def at(t):
    return slice(t * SUB, (t + 1) * SUB)


def lane_loop(chans, group):
    def step(g, _):
        group(pl.ds(pl.multiple_of(g * LANES, LANES), LANES))
        return 0

    lax.fori_loop(0, chans // LANES, step, 0)


def wide_rows(ref, lanes, modes):
    return [jnp.broadcast_to(ref[m : m + 1, lanes], (SUB, LANES)) for m in modes]


def run_states(decay, state, read, times):
    for t in times:
        now = read(t)
        state = [now] * len(decay) if state is None else [d * s + now for d, s in zip(decay, state)]
    return state


def bulk_kernel(
    tokens, x_hbm, taps_hbm, rate_hbm, head_ref, sig_ref, late_ref, taps_ref, rate_ref, x_ref, px_ref, sems
):
    rows = x_ref.shape[1]
    run = rows // SUB
    copies = [pltpu.make_async_copy(x_hbm.at[b + 1], x_ref.at[b], sems.at[b]) for b in range(2)]
    small = [
        pltpu.make_async_copy(taps_hbm, taps_ref, sems.at[2]),
        pltpu.make_async_copy(rate_hbm, rate_ref, sems.at[3]),
    ]
    for c in copies + small:
        c.start()
    move = spread_matrix(rows)
    for b, c in enumerate(copies):
        c.wait()
        moved = jnp.dot(move, x_ref[b], preferred_element_type=f32)
        px_ref[b] = moved
        head_ref[b] = moved[: 2 * BACK * SUB]
    for c in small:
        c.wait()

    def group(lanes):
        def put(t, v):
            sig_ref[at(t), lanes] = v

        def mul(t, v):
            sig_ref[at(t), lanes] = sig_ref[at(t), lanes] * v

        late = range(BACK, run)
        fir(taps_ref, 1, lambda e: px_ref[0, at(e), lanes], lanes, late, put)
        fir(taps_ref, 2, lambda e: px_ref[1, at(e), lanes], lanes, late, mul)
        decay = [jnp.exp(r * (-1.0 / tokens)) for r in wide_rows(rate_ref, lanes, range(MODES))]
        state = run_states(decay, None, lambda t: sig_ref[at(t), lanes], late)
        for m in range(MODES):
            late_ref[m, :, lanes] = state[m]

    lane_loop(x_ref.shape[2], group)


def edge_kernel(
    rows, tokens, head_ref, halo_ref, taps_ref, rate_ref, late_ref, early_ref, ends_ref, send_ref, edges, faded
):
    run = rows // SUB
    n_ctx = send_ref.shape[0]
    for b in (1, 2):
        edges[b - 1] = head_ref[b - 1, : BACK * SUB] + edge_rows(halo_ref, b)
    me = lax.axis_index("ctx")
    below = (SUB - 1 - lax.broadcasted_iota(jnp.int32, (SUB, LANES), 0)).astype(f32) * (-run / tokens)

    def group(lanes):
        def put(t, v):
            early_ref[at(t), lanes] = v

        def mul(t, v):
            early_ref[at(t), lanes] = early_ref[at(t), lanes] * v

        for b, emit in ((1, put), (2, mul)):
            fir(
                taps_ref,
                b,
                lambda e, b=b: edges[b - 1, at(e), lanes] if e < BACK else head_ref[b - 1, at(e), lanes],
                lanes,
                range(BACK),
                emit,
            )
        rate = wide_rows(rate_ref, lanes, range(MODES))
        decay = [jnp.exp(r * (-1.0 / tokens)) for r in rate]
        state = run_states(decay, None, lambda t: early_ref[at(t), lanes], range(BACK))
        for m in range(MODES):
            end = late_ref[m, :, lanes] + state[m] * jnp.exp(rate[m] * (-(run - BACK) / tokens))
            ends_ref[m, :, lanes] = end
            faded[m] = end * jnp.exp(rate[m] * below)
        total = jnp.sum(faded[...], axis=1)
        whole = jnp.exp(rate_ref[:, lanes] * (-rows / tokens))
        for d in range(n_ctx):
            send_ref[d, :, lanes] = jnp.where(d > me, total, 0.0).astype(bf16)
            total = jnp.where(d > me, total * whole, total)

    lane_loop(head_ref.shape[2], group)


def inner_kernel(
    tokens,
    x_hbm,
    weight_hbm,
    halo_ref,
    taps_ref,
    rate_ref,
    coef_ref,
    sig_ref,
    early_ref,
    ends_ref,
    q_ref,
    y_ref,
    lead_ref,
    turn_ref,
    weight_ref,
    x_ref,
    px_ref,
    half_ref,
    sems,
):
    copy = pltpu.make_async_copy(x_hbm.at[0], x_ref, sems.at[0])
    fetch = pltpu.make_async_copy(weight_hbm.at[:, : weight_ref.shape[1]], weight_ref, sems.at[1])
    copy.start()
    fetch.start()
    rows = q_ref.shape[0]
    run = rows // SUB
    move = spread_matrix(rows)
    copy.wait()
    px_ref[...] = jnp.dot(move, x_ref[...], preferred_element_type=f32)
    px_ref[: BACK * SUB] = px_ref[: BACK * SUB] + edge_rows(halo_ref, 0)
    sub = lax.broadcasted_iota(jnp.int32, (SUB, LANES), 0)
    sub_time = (sub * run + 1).astype(f32) * (-1.0 / tokens)

    def group(lanes):
        def put(t, v):
            q_ref[at(t), lanes] = v

        def signal(t):
            return early_ref[at(t), lanes] if t < BACK else sig_ref[at(t), lanes]

        fir(
            taps_ref,
            0,
            lambda e: px_ref[at(e), lanes],
            lanes,
            range(run),
            put,
        )
        for first in range(0, MODES, 8):
            modes = range(first, first + 8)
            coef = wide_rows(coef_ref, lanes, modes)
            rate = wide_rows(rate_ref, lanes, modes)
            decay = [jnp.exp(r * (-1.0 / tokens)) for r in rate]
            state = []
            for i, m in enumerate(modes):
                lead_ref[m, :, lanes] = coef[i] * jnp.exp(rate[i] * sub_time)
                s = ends_ref[m, :, lanes]
                for by in (1, 2, 4):
                    moved = jnp.where(sub >= by, pltpu.roll(s, by, 0), 0.0)
                    s = s + moved * jnp.exp(rate[i] * (-by * run / tokens))
                state.append(jnp.where(sub >= 1, pltpu.roll(s, 1, 0), 0.0))
            for t in range(run):
                state = run_states(decay, state, signal, [t])
                terms = [c * s for c, s in zip(coef, state)]
                while len(terms) > 1:
                    terms = [terms[i] + terms[i + 1] for i in range(0, len(terms), 2)]
                if first == 0:
                    half_ref[at(t), lanes] = terms[0]
                else:
                    y_ref[at(t), lanes] = half_ref[at(t), lanes] + terms[0]

    lane_loop(q_ref.shape[1], group)
    tp = lax.axis_index("tp")
    half, z = tp // NZ, tp % NZ
    way = 1 - 2 * (lax.axis_index("ctx") % 2)

    def natural(o):
        block = ((half + o // (NZ * 16)) % 2) * NZ + (z + way * (o // 16 % NZ) + NZ) % NZ
        n = block * 16 + o % 16
        return (n % run) * SUB + n // run

    turn_ref[...] = one_hot(rows, rows, natural)
    fetch.wait()


def column_copies(weight_hbm, weight, sems, base):
    tiles = sems.shape[0]
    tile = weight.shape[1] // tiles
    copies = []
    for i in range(tiles):
        here = slice(i * tile, (i + 1) * tile)
        there = slice(base + i * tile, base + (i + 1) * tile)
        copies.append((here, pltpu.make_async_copy(weight_hbm.at[:, there], weight.at[:, here], sems.at[i])))
    for _, copy in copies:
        copy.start()
    return copies


def times(left, copies, weight, out_ref, base=0):
    for here, copy in copies:
        copy.wait()
        out_ref[:, slice(base + here.start, base + here.stop)] = jnp.dot(left, weight[:, here], preferred_element_type=f32).astype(bf16)


def gate_kernel(
    tokens,
    weight_hbm,
    recv_ref,
    rate_ref,
    lead_ref,
    y_ref,
    q_ref,
    turn_ref,
    ready_ref,
    gated_ref,
    part_ref,
    flat,
    weight,
    sems,
):
    ready = ready_ref.shape[1]
    copies = column_copies(weight_hbm, weight, sems, ready)
    n_ctx = recv_ref.shape[0]
    run = y_ref.shape[0] // SUB

    def group(lanes):
        start = recv_ref[0, :, lanes].astype(f32)
        for p in range(1, n_ctx):
            start = start + recv_ref[p, :, lanes].astype(f32)
        state = [jnp.broadcast_to(start[m : m + 1], (SUB, LANES)) * lead_ref[m, :, lanes] for m in range(MODES)]
        decay = [jnp.exp(r * (-1.0 / tokens)) for r in wide_rows(rate_ref, lanes, range(MODES))]
        for t in range(run):
            terms = [y_ref[at(t), lanes]] + state
            while len(terms) > 1:
                terms = [terms[i] + terms[i + 1] for i in range(0, len(terms) - 1, 2)] + terms[len(terms) // 2 * 2 :]
            flat[at(t), lanes] = terms[0] * q_ref[at(t), lanes]
            if t < run - 1:
                state = [d * s for d, s in zip(decay, state)]

    lane_loop(y_ref.shape[1], group)
    gated = jnp.dot(turn_ref[...], flat[...].astype(bf16), preferred_element_type=f32).astype(bf16)
    gated_ref[...] = gated
    part_ref[:, :ready] = jnp.dot(gated, ready_ref[...], preferred_element_type=f32).astype(bf16)
    times(gated, copies, weight, part_ref, ready)


def project_kernel(base, weight_hbm, gated_ref, part_ref, weight, sems):
    copies = column_copies(weight_hbm, weight, sems, base)
    times(gated_ref[...], copies, weight, part_ref)


def ring_pairs(n_ctx, by):
    return [
        ((c * 2 + h) * NZ + z, (c * 2 + h) * NZ + (z + by * (1 - 2 * (c % 2))) % NZ)
        for c in range(n_ctx)
        for h in range(2)
        for z in range(NZ)
    ]


def half_pairs():
    return [(i, (i + NZ) % (2 * NZ)) for i in range(2 * NZ)]


def plus(*terms):
    return sum(t.astype(f32) for t in terms).astype(bf16)


def along(x, way):
    return lax.ppermute(x, ("ctx", "tp"), ring_pairs(lax.axis_size("ctx"), way))


def across(x):
    return lax.ppermute(x, "tp", half_pairs())


def reduce_columns(part, longer, meet):
    part = part.reshape(2, NZ, 16, -1)
    left = {longer: NZ // 2, -longer: NZ // 2 - 1}
    total = {way: part[:, way * k % NZ] for way, k in left.items()}
    for _ in range(NZ // 2 - meet):
        for way in left:
            if left[way] > meet:
                left[way] -= 1
                total[way] = along(total[way], way)
                if left[way]:
                    total[way] = plus(total[way], part[:, way * left[way] % NZ])
    if meet == 0:
        both = total[1].astype(f32) + total[-1].astype(f32) + part[:, 0].astype(f32)
        return plus(both[0], across(both[1].astype(bf16)))
    near = range(1 - meet, meet)
    got = across(jnp.stack([part[1, k % NZ] for k in near]))
    close = {k: plus(part[0, k % NZ], got[i]) for i, k in enumerate(near)}
    other = across(jnp.stack([total[1][1], total[-1][1]]))
    total = {1: plus(total[1][0], other[0]), -1: plus(total[-1][0], other[1])}
    for k in range(meet - 1, -1, -1):
        for way in total:
            total[way] = along(total[way], way)
            if k:
                total[way] = plus(total[way], close[way * k])
    return plus(total[1], total[-1], close[0])


def call(kernel, outs, scratch, name, flops, *args, far=(), aliases=None):
    in_specs = [pl.BlockSpec(memory_space=pl.ANY)] * len(far) + [pl.BlockSpec(memory_space=VMEM)] * len(args)
    args = [pltpu.with_memory_space_constraint(x, pltpu.HBM) for x in far] + [
        pltpu.with_memory_space_constraint(x, VMEM) for x in args
    ]
    return pl.pallas_call(
        kernel,
        in_specs=in_specs,
        out_specs=[pl.BlockSpec(memory_space=VMEM)] * len(outs),
        out_shape=[VMEM(s, d) for s, d in outs],
        scratch_shapes=[s if not isinstance(s, tuple) else VMEM(*s) for s in scratch],
        compiler_params=pltpu.CompilerParams(vmem_limit_bytes=16 * 2**20),
        input_output_aliases=aliases or {},
        cost_estimate=pl.CostEstimate(flops=flops, bytes_accessed=4 * 2**20, transcendentals=0),
        name=name,
    )(*args)


def local(features, short_filter, decay_rate, residue, out_weight):
    rows, _, chans = features.shape
    n_ctx = lax.axis_size("ctx")
    tokens = rows * n_ctx
    run = rows // SUB
    halo = lax.ppermute(features[rows - HALO :], "ctx", [(i, i + 1) for i in range(n_ctx - 1)])
    halo = jnp.transpose(halo, (1, 0, 2))
    x = jnp.transpose(features, (1, 0, 2))
    wide = ((rows, chans), f32)
    states = ((MODES, SUB, chans), f32)
    moved = ((run + BACK) * SUB, chans)
    head = 2 * BACK * SUB
    heads, sig, late, taps, rate = call(
        functools.partial(bulk_kernel, tokens),
        [((2, head, chans), f32), wide, states, (short_filter.shape, f32), (decay_rate.shape, f32)],
        [((2, rows, chans), bf16), ((2, *moved), f32), pltpu.SemaphoreType.DMA((4,))],
        "bulk",
        4 * rows * chans * MODES,
        far=(x, short_filter, decay_rate),
    )
    early, ends, send = call(
        functools.partial(edge_kernel, rows, tokens),
        [((BACK * SUB, chans), f32), states, ((n_ctx, MODES, chans), bf16)],
        [((2, BACK * SUB, chans), f32), ((MODES, SUB, LANES), f32)],
        "edge",
        rows * chans * MODES,
        heads,
        halo,
        taps,
        rate,
        late,
    )
    recv = lax.all_to_all(send, "ctx", 0, 0, tiled=True)
    late_rate, late_residue, _ = lax.optimization_barrier((decay_rate, residue, early))
    coef = late_residue * jnp.sqrt(1.0 / tokens - jnp.expm1(late_rate * (-2.0 / tokens)))
    q, y, lead, turn, ready = call(
        functools.partial(inner_kernel, tokens),
        [wide, wide, states, ((rows, rows), bf16), ((chans, READY), bf16)],
        [((rows, chans), bf16), (moved, f32), wide, pltpu.SemaphoreType.DMA((2,))],
        "inner",
        8 * rows * chans * MODES,
        halo,
        taps,
        rate,
        coef,
        sig,
        early,
        ends,
        far=(x, out_weight),
        aliases={6: 1},
    )

    def stream(width):
        return [((chans, width), bf16), pltpu.SemaphoreType.DMA((max(width // 1024, 1),))]

    gated, first = call(
        functools.partial(gate_kernel, tokens),
        [((rows, chans), bf16), ((rows, WIDTHS[0]), bf16)],
        [wide, *stream(WIDTHS[0] - READY)],
        "gate",
        2 * rows * chans * WIDTHS[0],
        recv,
        rate,
        lead,
        y,
        q,
        turn,
        ready,
        far=(out_weight,),
    )
    parts, base = [first], WIDTHS[0]
    for width in WIDTHS[1:]:
        parts += call(
            functools.partial(project_kernel, base),
            [((rows, width), bf16)],
            stream(width),
            "project",
            2 * rows * chans * width,
            gated,
            far=(out_weight,),
        )
        base += width
    return jnp.concatenate([reduce_columns(p, 1, m) for p, m in zip(parts, MEET)], axis=1)


def solution(mesh):
    in_specs = (
        P("ctx", None, "tp"),
        P(None, None, "tp"),
        P(None, "tp"),
        P(None, "tp"),
        P("tp", None),
    )
    out_specs = P(("ctx", "tp"), None)
    return jax.shard_map(local, mesh=mesh, in_specs=in_specs, out_specs=out_specs, check_vma=False)
```

```python
import functools

import jax
import jax.numpy as jnp
from jax import lax
from jax.experimental import pallas as pl
from jax.experimental.pallas import tpu as pltpu
from jax.sharding import PartitionSpec as P

TAPS = 7
MODES = 16
SUB = 8
LANES = 128
NZ = 8
HALO = 16
READY = 1024
MEET = (2, 0)
WIDTHS = (4096, 4096)
BACK = TAPS - 1

f32 = jnp.float32
bf16 = jnp.bfloat16
VMEM = pltpu.VMEM


def one_hot(rows, cols, pick):
    row = lax.broadcasted_iota(jnp.int32, (rows, LANES), 0)
    want = pick(row)
    col = lax.broadcasted_iota(jnp.int32, (rows, LANES), 1)
    tiles = [jnp.where(want == col + c, 1.0, 0.0).astype(bf16) for c in range(0, cols, LANES)]
    return jnp.concatenate(tiles, axis=1)


def spread_matrix(rows):
    run = rows // SUB
    return one_hot((run + BACK) * SUB, rows, lambda r: run * (r % SUB) + r // SUB - BACK)


def edge_rows(halo_ref, branch):
    first = one_hot(BACK * SUB, LANES, lambda r: jnp.where(r % SUB == 0, r // SUB + HALO - BACK, -1))[:, :HALO]
    return jnp.dot(first, halo_ref[branch], preferred_element_type=f32)


def fir(taps_ref, branch, read, lanes, times, emit):
    taps = [jnp.broadcast_to(taps_ref[branch, j : j + 1, lanes], (SUB, LANES)) for j in range(TAPS)]
    window = [read(times[0] + e) for e in range(BACK)][::-1]
    for t in times:
        window = [read(t + BACK)] + window
        terms = [taps[j] * window[j] for j in range(TAPS)]
        while len(terms) > 1:
            terms = [terms[i] + terms[i + 1] for i in range(0, len(terms) - 1, 2)] + terms[len(terms) // 2 * 2 :]
        emit(t, terms[0])
        window = window[:BACK]


def at(t):
    return slice(t * SUB, (t + 1) * SUB)


def lane_loop(chans, group):
    def step(g, _):
        group(pl.ds(pl.multiple_of(g * LANES, LANES), LANES))
        return 0

    lax.fori_loop(0, chans // LANES, step, 0)


def wide_rows(ref, lanes, modes):
    return [jnp.broadcast_to(ref[m : m + 1, lanes], (SUB, LANES)) for m in modes]


def run_states(decay, state, read, times):
    for t in times:
        now = read(t)
        state = [now] * len(decay) if state is None else [d * s + now for d, s in zip(decay, state)]
    return state


def bulk_kernel(
    tokens, x_hbm, taps_hbm, rate_hbm, head_ref, sig_ref, late_ref, taps_ref, rate_ref, x_ref, px_ref, sems
):
    rows = x_ref.shape[1]
    run = rows // SUB
    copies = [pltpu.make_async_copy(x_hbm.at[b + 1], x_ref.at[b], sems.at[b]) for b in range(2)]
    small = [
        pltpu.make_async_copy(taps_hbm, taps_ref, sems.at[2]),
        pltpu.make_async_copy(rate_hbm, rate_ref, sems.at[3]),
    ]
    for c in copies + small:
        c.start()
    move = spread_matrix(rows)
    for b, c in enumerate(copies):
        c.wait()
        moved = jnp.dot(move, x_ref[b], preferred_element_type=f32)
        px_ref[b] = moved
        head_ref[b] = moved[: 2 * BACK * SUB]
    for c in small:
        c.wait()

    def group(lanes):
        def put(t, v):
            sig_ref[at(t), lanes] = v

        def mul(t, v):
            sig_ref[at(t), lanes] = sig_ref[at(t), lanes] * v

        late = range(BACK, run)
        fir(taps_ref, 1, lambda e: px_ref[0, at(e), lanes], lanes, late, put)
        fir(taps_ref, 2, lambda e: px_ref[1, at(e), lanes], lanes, late, mul)
        decay = [jnp.exp(r * (-1.0 / tokens)) for r in wide_rows(rate_ref, lanes, range(MODES))]
        state = run_states(decay, None, lambda t: sig_ref[at(t), lanes], late)
        for m in range(MODES):
            late_ref[m, :, lanes] = state[m]

    lane_loop(x_ref.shape[2], group)


def edge_kernel(
    rows, tokens, head_ref, halo_ref, taps_ref, rate_ref, late_ref, early_ref, ends_ref, send_ref, edges, faded
):
    run = rows // SUB
    n_ctx = send_ref.shape[0]
    for b in (1, 2):
        edges[b - 1] = head_ref[b - 1, : BACK * SUB] + edge_rows(halo_ref, b)
    me = lax.axis_index("ctx")
    below = (SUB - 1 - lax.broadcasted_iota(jnp.int32, (SUB, LANES), 0)).astype(f32) * (-run / tokens)

    def group(lanes):
        def put(t, v):
            early_ref[at(t), lanes] = v

        def mul(t, v):
            early_ref[at(t), lanes] = early_ref[at(t), lanes] * v

        for b, emit in ((1, put), (2, mul)):
            fir(
                taps_ref,
                b,
                lambda e, b=b: edges[b - 1, at(e), lanes] if e < BACK else head_ref[b - 1, at(e), lanes],
                lanes,
                range(BACK),
                emit,
            )
        rate = wide_rows(rate_ref, lanes, range(MODES))
        decay = [jnp.exp(r * (-1.0 / tokens)) for r in rate]
        state = run_states(decay, None, lambda t: early_ref[at(t), lanes], range(BACK))
        for m in range(MODES):
            end = late_ref[m, :, lanes] + state[m] * jnp.exp(rate[m] * (-(run - BACK) / tokens))
            ends_ref[m, :, lanes] = end
            faded[m] = end * jnp.exp(rate[m] * below)
        total = jnp.sum(faded[...], axis=1)
        whole = jnp.exp(rate_ref[:, lanes] * (-rows / tokens))
        for d in range(n_ctx):
            send_ref[d, :, lanes] = jnp.where(d > me, total, 0.0).astype(bf16)
            total = jnp.where(d > me, total * whole, total)

    lane_loop(head_ref.shape[2], group)


def inner_kernel(
    tokens,
    x_hbm,
    weight_hbm,
    halo_ref,
    taps_ref,
    rate_ref,
    coef_ref,
    sig_ref,
    early_ref,
    ends_ref,
    q_ref,
    y_ref,
    lead_ref,
    turn_ref,
    weight_ref,
    x_ref,
    px_ref,
    half_ref,
    sems,
):
    copy = pltpu.make_async_copy(x_hbm.at[0], x_ref, sems.at[0])
    fetch = pltpu.make_async_copy(weight_hbm.at[:, : weight_ref.shape[1]], weight_ref, sems.at[1])
    copy.start()
    fetch.start()
    rows = q_ref.shape[0]
    run = rows // SUB
    move = spread_matrix(rows)
    copy.wait()
    px_ref[...] = jnp.dot(move, x_ref[...], preferred_element_type=f32)
    px_ref[: BACK * SUB] = px_ref[: BACK * SUB] + edge_rows(halo_ref, 0)
    sub = lax.broadcasted_iota(jnp.int32, (SUB, LANES), 0)
    sub_time = (sub * run + 1).astype(f32) * (-1.0 / tokens)

    def group(lanes):
        def put(t, v):
            q_ref[at(t), lanes] = v

        def signal(t):
            return early_ref[at(t), lanes] if t < BACK else sig_ref[at(t), lanes]

        fir(
            taps_ref,
            0,
            lambda e: px_ref[at(e), lanes],
            lanes,
            range(run),
            put,
        )
        for first in range(0, MODES, 8):
            modes = range(first, first + 8)
            coef = wide_rows(coef_ref, lanes, modes)
            rate = wide_rows(rate_ref, lanes, modes)
            decay = [jnp.exp(r * (-1.0 / tokens)) for r in rate]
            state = []
            for i, m in enumerate(modes):
                lead_ref[m, :, lanes] = coef[i] * jnp.exp(rate[i] * sub_time)
                s = ends_ref[m, :, lanes]
                for by in (1, 2, 4):
                    moved = jnp.where(sub >= by, pltpu.roll(s, by, 0), 0.0)
                    s = s + moved * jnp.exp(rate[i] * (-by * run / tokens))
                state.append(jnp.where(sub >= 1, pltpu.roll(s, 1, 0), 0.0))
            for t in range(run):
                state = run_states(decay, state, signal, [t])
                terms = [c * s for c, s in zip(coef, state)]
                while len(terms) > 1:
                    terms = [terms[i] + terms[i + 1] for i in range(0, len(terms), 2)]
                if first == 0:
                    half_ref[at(t), lanes] = terms[0]
                else:
                    y_ref[at(t), lanes] = half_ref[at(t), lanes] + terms[0]

    lane_loop(q_ref.shape[1], group)
    tp = lax.axis_index("tp")
    half, z = tp // NZ, tp % NZ
    way = 1 - 2 * (lax.axis_index("ctx") % 2)

    def natural(o):
        block = ((half + o // (NZ * 16)) % 2) * NZ + (z + way * (o // 16 % NZ) + NZ) % NZ
        n = block * 16 + o % 16
        return (n % run) * SUB + n // run

    turn_ref[...] = one_hot(rows, rows, natural)
    fetch.wait()


def column_copies(weight_hbm, weight, sems, base):
    tiles = sems.shape[0]
    tile = weight.shape[1] // tiles
    copies = []
    for i in range(tiles):
        here = slice(i * tile, (i + 1) * tile)
        there = slice(base + i * tile, base + (i + 1) * tile)
        copies.append((here, pltpu.make_async_copy(weight_hbm.at[:, there], weight.at[:, here], sems.at[i])))
    for _, copy in copies:
        copy.start()
    return copies


def times(left, copies, weight, out_ref, base=0):
    for here, copy in copies:
        copy.wait()
        out_ref[:, slice(base + here.start, base + here.stop)] = jnp.dot(left, weight[:, here], preferred_element_type=f32).astype(bf16)


def gate_kernel(
    tokens,
    weight_hbm,
    recv_ref,
    rate_ref,
    lead_ref,
    y_ref,
    q_ref,
    turn_ref,
    ready_ref,
    gated_ref,
    part_ref,
    flat,
    weight,
    sems,
):
    ready = ready_ref.shape[1]
    copies = column_copies(weight_hbm, weight, sems, ready)
    n_ctx = recv_ref.shape[0]
    run = y_ref.shape[0] // SUB

    def group(lanes):
        start = recv_ref[0, :, lanes].astype(f32)
        for p in range(1, n_ctx):
            start = start + recv_ref[p, :, lanes].astype(f32)
        state = [jnp.broadcast_to(start[m : m + 1], (SUB, LANES)) * lead_ref[m, :, lanes] for m in range(MODES)]
        decay = [jnp.exp(r * (-1.0 / tokens)) for r in wide_rows(rate_ref, lanes, range(MODES))]
        for t in range(run):
            terms = [y_ref[at(t), lanes]] + state
            while len(terms) > 1:
                terms = [terms[i] + terms[i + 1] for i in range(0, len(terms) - 1, 2)] + terms[len(terms) // 2 * 2 :]
            flat[at(t), lanes] = terms[0] * q_ref[at(t), lanes]
            if t < run - 1:
                state = [d * s for d, s in zip(decay, state)]

    lane_loop(y_ref.shape[1], group)
    gated = jnp.dot(turn_ref[...], flat[...].astype(bf16), preferred_element_type=f32).astype(bf16)
    gated_ref[...] = gated
    part_ref[:, :ready] = jnp.dot(gated, ready_ref[...], preferred_element_type=f32).astype(bf16)
    times(gated, copies, weight, part_ref, ready)


def project_kernel(base, weight_hbm, gated_ref, part_ref, weight, sems):
    copies = column_copies(weight_hbm, weight, sems, base)
    times(gated_ref[...], copies, weight, part_ref)


def ring_pairs(n_ctx, by):
    return [
        ((c * 2 + h) * NZ + z, (c * 2 + h) * NZ + (z + by * (1 - 2 * (c % 2))) % NZ)
        for c in range(n_ctx)
        for h in range(2)
        for z in range(NZ)
    ]


def half_pairs():
    return [(i, (i + NZ) % (2 * NZ)) for i in range(2 * NZ)]


def plus(*terms):
    return sum(t.astype(f32) for t in terms).astype(bf16)


def along(x, way):
    return lax.ppermute(x, ("ctx", "tp"), ring_pairs(lax.axis_size("ctx"), way))


def across(x):
    return lax.ppermute(x, "tp", half_pairs())


def reduce_columns(part, longer, meet):
    part = part.reshape(2, NZ, 16, -1)
    left = {longer: NZ // 2, -longer: NZ // 2 - 1}
    total = {way: part[:, way * k % NZ] for way, k in left.items()}
    near = range(1 - meet, meet)
    got = None
    for _ in range(NZ // 2 - meet):
        for way in left:
            if left[way] > meet:
                left[way] -= 1
                total[way] = along(total[way], way)
                if left[way]:
                    total[way] = plus(total[way], part[:, way * left[way] % NZ])
        if meet and got is None:
            mine = jnp.stack([part[1, k % NZ] for k in near])
            got = across(lax.optimization_barrier((mine, total[-longer]))[0])
    if meet == 0:
        both = total[1].astype(f32) + total[-1].astype(f32) + part[:, 0].astype(f32)
        return plus(both[0], across(both[1].astype(bf16)))
    close = {k: plus(part[0, k % NZ], got[i]) for i, k in enumerate(near)}
    other = across(jnp.stack([total[1][1], total[-1][1]]))
    total = {1: plus(total[1][0], other[0]), -1: plus(total[-1][0], other[1])}
    for k in range(meet - 1, -1, -1):
        for way in total:
            total[way] = along(total[way], way)
            if k:
                total[way] = plus(total[way], close[way * k])
    return plus(total[1], total[-1], close[0])


def call(kernel, outs, scratch, name, flops, *args, far=(), aliases=None):
    in_specs = [pl.BlockSpec(memory_space=pl.ANY)] * len(far) + [pl.BlockSpec(memory_space=VMEM)] * len(args)
    args = [pltpu.with_memory_space_constraint(x, pltpu.HBM) for x in far] + [
        pltpu.with_memory_space_constraint(x, VMEM) for x in args
    ]
    return pl.pallas_call(
        kernel,
        in_specs=in_specs,
        out_specs=[pl.BlockSpec(memory_space=VMEM)] * len(outs),
        out_shape=[VMEM(s, d) for s, d in outs],
        scratch_shapes=[s if not isinstance(s, tuple) else VMEM(*s) for s in scratch],
        compiler_params=pltpu.CompilerParams(vmem_limit_bytes=16 * 2**20),
        input_output_aliases=aliases or {},
        cost_estimate=pl.CostEstimate(flops=flops, bytes_accessed=4 * 2**20, transcendentals=0),
        name=name,
    )(*args)


def local(features, short_filter, decay_rate, residue, out_weight):
    rows, _, chans = features.shape
    n_ctx = lax.axis_size("ctx")
    tokens = rows * n_ctx
    run = rows // SUB
    halo = lax.ppermute(features[rows - HALO :], "ctx", [(i, i + 1) for i in range(n_ctx - 1)])
    halo = jnp.transpose(halo, (1, 0, 2))
    x = jnp.transpose(features, (1, 0, 2))
    wide = ((rows, chans), f32)
    states = ((MODES, SUB, chans), f32)
    moved = ((run + BACK) * SUB, chans)
    head = 2 * BACK * SUB
    heads, sig, late, taps, rate = call(
        functools.partial(bulk_kernel, tokens),
        [((2, head, chans), f32), wide, states, (short_filter.shape, f32), (decay_rate.shape, f32)],
        [((2, rows, chans), bf16), ((2, *moved), f32), pltpu.SemaphoreType.DMA((4,))],
        "bulk",
        4 * rows * chans * MODES,
        far=(x, short_filter, decay_rate),
    )
    early, ends, send = call(
        functools.partial(edge_kernel, rows, tokens),
        [((BACK * SUB, chans), f32), states, ((n_ctx, MODES, chans), bf16)],
        [((2, BACK * SUB, chans), f32), ((MODES, SUB, LANES), f32)],
        "edge",
        rows * chans * MODES,
        heads,
        halo,
        taps,
        rate,
        late,
    )
    recv = lax.all_to_all(send, "ctx", 0, 0, tiled=True)
    late_rate, late_residue, _ = lax.optimization_barrier((decay_rate, residue, early))
    coef = late_residue * jnp.sqrt(1.0 / tokens - jnp.expm1(late_rate * (-2.0 / tokens)))
    q, y, lead, turn, ready = call(
        functools.partial(inner_kernel, tokens),
        [wide, wide, states, ((rows, rows), bf16), ((chans, READY), bf16)],
        [((rows, chans), bf16), (moved, f32), wide, pltpu.SemaphoreType.DMA((2,))],
        "inner",
        8 * rows * chans * MODES,
        halo,
        taps,
        rate,
        coef,
        sig,
        early,
        ends,
        far=(x, out_weight),
        aliases={6: 1},
    )

    def stream(width):
        return [((chans, width), bf16), pltpu.SemaphoreType.DMA((max(width // 1024, 1),))]

    gated, first = call(
        functools.partial(gate_kernel, tokens),
        [((rows, chans), bf16), ((rows, WIDTHS[0]), bf16)],
        [wide, *stream(WIDTHS[0] - READY)],
        "gate",
        2 * rows * chans * WIDTHS[0],
        recv,
        rate,
        lead,
        y,
        q,
        turn,
        ready,
        far=(out_weight,),
    )
    parts, base = [first], WIDTHS[0]
    for width in WIDTHS[1:]:
        parts += call(
            functools.partial(project_kernel, base),
            [((rows, width), bf16)],
            stream(width),
            "project",
            2 * rows * chans * width,
            gated,
            far=(out_weight,),
        )
        base += width
    return jnp.concatenate([reduce_columns(p, 1, m) for p, m in zip(parts, MEET)], axis=1)


def solution(mesh):
    in_specs = (
        P("ctx", None, "tp"),
        P(None, None, "tp"),
        P(None, "tp"),
        P(None, "tp"),
        P("tp", None),
    )
    out_specs = P(("ctx", "tp"), None)
    return jax.shard_map(local, mesh=mesh, in_specs=in_specs, out_specs=out_specs, check_vma=False)
```

```python
import functools

import jax
import jax.numpy as jnp
from jax import lax
from jax.experimental import pallas as pl
from jax.experimental.pallas import tpu as pltpu
from jax.sharding import PartitionSpec as P

TAPS = 7
MODES = 16
SUB = 8
LANES = 128
NZ = 8
HALO = 16
READY = 1024
MEET = (2, 0)
WIDTHS = (4096, 4096)
BACK = TAPS - 1

f32 = jnp.float32
bf16 = jnp.bfloat16
VMEM = pltpu.VMEM


def one_hot(rows, cols, pick):
    row = lax.broadcasted_iota(jnp.int32, (rows, LANES), 0)
    want = pick(row)
    col = lax.broadcasted_iota(jnp.int32, (rows, LANES), 1)
    tiles = [jnp.where(want == col + c, 1.0, 0.0).astype(bf16) for c in range(0, cols, LANES)]
    return jnp.concatenate(tiles, axis=1)


def spread_matrix(rows):
    run = rows // SUB
    return one_hot((run + BACK) * SUB, rows, lambda r: run * (r % SUB) + r // SUB - BACK)


def edge_rows(halo_ref, branch):
    first = one_hot(BACK * SUB, LANES, lambda r: jnp.where(r % SUB == 0, r // SUB + HALO - BACK, -1))[:, :HALO]
    return jnp.dot(first, halo_ref[branch], preferred_element_type=f32)


def fir(taps_ref, branch, read, lanes, times, emit):
    taps = [jnp.broadcast_to(taps_ref[branch, j : j + 1, lanes], (SUB, LANES)) for j in range(TAPS)]
    window = [read(times[0] + e) for e in range(BACK)][::-1]
    for t in times:
        window = [read(t + BACK)] + window
        terms = [taps[j] * window[j] for j in range(TAPS)]
        while len(terms) > 1:
            terms = [terms[i] + terms[i + 1] for i in range(0, len(terms) - 1, 2)] + terms[len(terms) // 2 * 2 :]
        emit(t, terms[0])
        window = window[:BACK]


def at(t):
    return slice(t * SUB, (t + 1) * SUB)


def lane_loop(chans, group):
    def step(g, _):
        group(pl.ds(pl.multiple_of(g * LANES, LANES), LANES))
        return 0

    lax.fori_loop(0, chans // LANES, step, 0)


def wide_rows(ref, lanes, modes):
    return [jnp.broadcast_to(ref[m : m + 1, lanes], (SUB, LANES)) for m in modes]


def run_states(decay, state, read, times):
    for t in times:
        now = read(t)
        state = [now] * len(decay) if state is None else [d * s + now for d, s in zip(decay, state)]
    return state


def bulk_kernel(
    tokens, x_hbm, taps_hbm, rate_hbm, head_ref, sig_ref, late_ref, taps_ref, rate_ref, x_ref, px_ref, sems
):
    rows = x_ref.shape[1]
    run = rows // SUB
    copies = [pltpu.make_async_copy(x_hbm.at[b + 1], x_ref.at[b], sems.at[b]) for b in range(2)]
    small = [
        pltpu.make_async_copy(taps_hbm, taps_ref, sems.at[2]),
        pltpu.make_async_copy(rate_hbm, rate_ref, sems.at[3]),
    ]
    for c in copies + small:
        c.start()
    move = spread_matrix(rows)
    for b, c in enumerate(copies):
        c.wait()
        moved = jnp.dot(move, x_ref[b], preferred_element_type=f32)
        px_ref[b] = moved
        head_ref[b] = moved[: 2 * BACK * SUB]
    for c in small:
        c.wait()

    def group(lanes):
        def put(t, v):
            sig_ref[at(t), lanes] = v

        def mul(t, v):
            sig_ref[at(t), lanes] = sig_ref[at(t), lanes] * v

        late = range(BACK, run)
        fir(taps_ref, 1, lambda e: px_ref[0, at(e), lanes], lanes, late, put)
        fir(taps_ref, 2, lambda e: px_ref[1, at(e), lanes], lanes, late, mul)
        decay = [jnp.exp(r * (-1.0 / tokens)) for r in wide_rows(rate_ref, lanes, range(MODES))]
        state = run_states(decay, None, lambda t: sig_ref[at(t), lanes], late)
        for m in range(MODES):
            late_ref[m, :, lanes] = state[m]

    lane_loop(x_ref.shape[2], group)


def edge_kernel(
    rows, tokens, head_ref, halo_ref, taps_ref, rate_ref, late_ref, early_ref, ends_ref, send_ref, edges, faded
):
    run = rows // SUB
    n_ctx = send_ref.shape[0]
    for b in (1, 2):
        edges[b - 1] = head_ref[b - 1, : BACK * SUB] + edge_rows(halo_ref, b)
    me = lax.axis_index("ctx")
    below = (SUB - 1 - lax.broadcasted_iota(jnp.int32, (SUB, LANES), 0)).astype(f32) * (-run / tokens)

    def group(lanes):
        def put(t, v):
            early_ref[at(t), lanes] = v

        def mul(t, v):
            early_ref[at(t), lanes] = early_ref[at(t), lanes] * v

        for b, emit in ((1, put), (2, mul)):
            fir(
                taps_ref,
                b,
                lambda e, b=b: edges[b - 1, at(e), lanes] if e < BACK else head_ref[b - 1, at(e), lanes],
                lanes,
                range(BACK),
                emit,
            )
        rate = wide_rows(rate_ref, lanes, range(MODES))
        decay = [jnp.exp(r * (-1.0 / tokens)) for r in rate]
        state = run_states(decay, None, lambda t: early_ref[at(t), lanes], range(BACK))
        for m in range(MODES):
            end = late_ref[m, :, lanes] + state[m] * jnp.exp(rate[m] * (-(run - BACK) / tokens))
            ends_ref[m, :, lanes] = end
            faded[m] = end * jnp.exp(rate[m] * below)
        total = jnp.sum(faded[...], axis=1)
        whole = jnp.exp(rate_ref[:, lanes] * (-rows / tokens))
        for d in range(n_ctx):
            send_ref[d, :, lanes] = jnp.where(d > me, total, 0.0).astype(bf16)
            total = jnp.where(d > me, total * whole, total)

    lane_loop(head_ref.shape[2], group)


def inner_kernel(
    tokens,
    x_hbm,
    weight_hbm,
    halo_ref,
    taps_ref,
    rate_ref,
    coef_ref,
    sig_ref,
    early_ref,
    ends_ref,
    q_ref,
    y_ref,
    lead_ref,
    turn_ref,
    weight_ref,
    x_ref,
    px_ref,
    half_ref,
    sems,
):
    copy = pltpu.make_async_copy(x_hbm.at[0], x_ref, sems.at[0])
    fetch = pltpu.make_async_copy(weight_hbm.at[:, : weight_ref.shape[1]], weight_ref, sems.at[1])
    copy.start()
    fetch.start()
    rows = q_ref.shape[0]
    run = rows // SUB
    move = spread_matrix(rows)
    copy.wait()
    px_ref[...] = jnp.dot(move, x_ref[...], preferred_element_type=f32)
    px_ref[: BACK * SUB] = px_ref[: BACK * SUB] + edge_rows(halo_ref, 0)
    sub = lax.broadcasted_iota(jnp.int32, (SUB, LANES), 0)
    sub_time = (sub * run + 1).astype(f32) * (-1.0 / tokens)

    def group(lanes):
        def put(t, v):
            q_ref[at(t), lanes] = v

        def signal(t):
            return early_ref[at(t), lanes] if t < BACK else sig_ref[at(t), lanes]

        fir(
            taps_ref,
            0,
            lambda e: px_ref[at(e), lanes],
            lanes,
            range(run),
            put,
        )
        for first in range(0, MODES, 8):
            modes = range(first, first + 8)
            coef = wide_rows(coef_ref, lanes, modes)
            rate = wide_rows(rate_ref, lanes, modes)
            decay = [jnp.exp(r * (-1.0 / tokens)) for r in rate]
            state = []
            for i, m in enumerate(modes):
                lead_ref[m, :, lanes] = coef[i] * jnp.exp(rate[i] * sub_time)
                s = ends_ref[m, :, lanes]
                for by in (1, 2, 4):
                    moved = jnp.where(sub >= by, pltpu.roll(s, by, 0), 0.0)
                    s = s + moved * jnp.exp(rate[i] * (-by * run / tokens))
                state.append(jnp.where(sub >= 1, pltpu.roll(s, 1, 0), 0.0))
            for t in range(run):
                state = run_states(decay, state, signal, [t])
                terms = [c * s for c, s in zip(coef, state)]
                while len(terms) > 1:
                    terms = [terms[i] + terms[i + 1] for i in range(0, len(terms), 2)]
                if first == 0:
                    half_ref[at(t), lanes] = terms[0]
                else:
                    y_ref[at(t), lanes] = half_ref[at(t), lanes] + terms[0]

    lane_loop(q_ref.shape[1], group)
    tp = lax.axis_index("tp")
    half, z = tp // NZ, tp % NZ
    way = 1 - 2 * (lax.axis_index("ctx") % 2)

    def natural(o):
        block = ((half + o // (NZ * 16)) % 2) * NZ + (z + way * (o // 16 % NZ) + NZ) % NZ
        n = block * 16 + o % 16
        return (n % run) * SUB + n // run

    turn_ref[...] = one_hot(rows, rows, natural)
    fetch.wait()


def column_copies(weight_hbm, weight, sems, base):
    tiles = sems.shape[0]
    tile = weight.shape[1] // tiles
    copies = []
    for i in range(tiles):
        here = slice(i * tile, (i + 1) * tile)
        there = slice(base + i * tile, base + (i + 1) * tile)
        copies.append((here, pltpu.make_async_copy(weight_hbm.at[:, there], weight.at[:, here], sems.at[i])))
    for _, copy in copies:
        copy.start()
    return copies


def times(left, copies, weight, out_ref, base=0):
    for here, copy in copies:
        copy.wait()
        out_ref[:, slice(base + here.start, base + here.stop)] = jnp.dot(left, weight[:, here], preferred_element_type=f32).astype(bf16)


def gate_kernel(
    tokens,
    weight_hbm,
    recv_ref,
    rate_ref,
    lead_ref,
    y_ref,
    q_ref,
    turn_ref,
    ready_ref,
    gated_ref,
    part_ref,
    ahead_ref,
    flat,
    weight,
    sems,
    ahead_sem,
):
    ready = ready_ref.shape[1]
    copies = column_copies(weight_hbm, weight, sems, ready)
    n_ctx = recv_ref.shape[0]
    run = y_ref.shape[0] // SUB

    def group(lanes):
        start = recv_ref[0, :, lanes].astype(f32)
        for p in range(1, n_ctx):
            start = start + recv_ref[p, :, lanes].astype(f32)
        state = [jnp.broadcast_to(start[m : m + 1], (SUB, LANES)) * lead_ref[m, :, lanes] for m in range(MODES)]
        decay = [jnp.exp(r * (-1.0 / tokens)) for r in wide_rows(rate_ref, lanes, range(MODES))]
        for t in range(run):
            terms = [y_ref[at(t), lanes]] + state
            while len(terms) > 1:
                terms = [terms[i] + terms[i + 1] for i in range(0, len(terms) - 1, 2)] + terms[len(terms) // 2 * 2 :]
            flat[at(t), lanes] = terms[0] * q_ref[at(t), lanes]
            if t < run - 1:
                state = [d * s for d, s in zip(decay, state)]

    lane_loop(y_ref.shape[1], group)
    gated = jnp.dot(turn_ref[...], flat[...].astype(bf16), preferred_element_type=f32).astype(bf16)
    gated_ref[...] = gated
    first = part_ref.shape[1]
    ahead = pltpu.make_async_copy(weight_hbm.at[:, first : first + ahead_ref.shape[1]], ahead_ref, ahead_sem)
    ahead.start()
    part_ref[:, :ready] = jnp.dot(gated, ready_ref[...], preferred_element_type=f32).astype(bf16)
    times(gated, copies, weight, part_ref, ready)
    ahead.wait()


def project_kernel(base, weight_hbm, gated_ref, ahead_ref, part_ref, weight, sems):
    ahead = ahead_ref.shape[1]
    copies = column_copies(weight_hbm, weight, sems, base + ahead)
    part_ref[:, :ahead] = jnp.dot(gated_ref[...], ahead_ref[...], preferred_element_type=f32).astype(bf16)
    times(gated_ref[...], copies, weight, part_ref, ahead)


def ring_pairs(n_ctx, by):
    return [
        ((c * 2 + h) * NZ + z, (c * 2 + h) * NZ + (z + by * (1 - 2 * (c % 2))) % NZ)
        for c in range(n_ctx)
        for h in range(2)
        for z in range(NZ)
    ]


def half_pairs():
    return [(i, (i + NZ) % (2 * NZ)) for i in range(2 * NZ)]


def plus(*terms):
    return sum(t.astype(f32) for t in terms).astype(bf16)


def along(x, way):
    return lax.ppermute(x, ("ctx", "tp"), ring_pairs(lax.axis_size("ctx"), way))


def across(x):
    return lax.ppermute(x, "tp", half_pairs())


def reduce_columns(part, longer, meet):
    part = part.reshape(2, NZ, 16, -1)
    left = {longer: NZ // 2, -longer: NZ // 2 - 1}
    total = {way: part[:, way * k % NZ] for way, k in left.items()}
    near = range(1 - meet, meet)
    got = None
    for _ in range(NZ // 2 - meet):
        for way in left:
            if left[way] > meet:
                left[way] -= 1
                total[way] = along(total[way], way)
                if left[way]:
                    total[way] = plus(total[way], part[:, way * left[way] % NZ])
        if meet and got is None:
            mine = jnp.stack([part[1, k % NZ] for k in near])
            got = across(lax.optimization_barrier((mine, total[-longer]))[0])
    if meet == 0:
        both = total[1].astype(f32) + total[-1].astype(f32) + part[:, 0].astype(f32)
        return plus(both[0], across(both[1].astype(bf16)))
    close = {k: plus(part[0, k % NZ], got[i]) for i, k in enumerate(near)}
    other = across(jnp.stack([total[1][1], total[-1][1]]))
    total = {1: plus(total[1][0], other[0]), -1: plus(total[-1][0], other[1])}
    for k in range(meet - 1, -1, -1):
        for way in total:
            total[way] = along(total[way], way)
            if k:
                total[way] = plus(total[way], close[way * k])
    return plus(total[1], total[-1], close[0])


def call(kernel, outs, scratch, name, flops, *args, far=(), aliases=None):
    in_specs = [pl.BlockSpec(memory_space=pl.ANY)] * len(far) + [pl.BlockSpec(memory_space=VMEM)] * len(args)
    args = [pltpu.with_memory_space_constraint(x, pltpu.HBM) for x in far] + [
        pltpu.with_memory_space_constraint(x, VMEM) for x in args
    ]
    return pl.pallas_call(
        kernel,
        in_specs=in_specs,
        out_specs=[pl.BlockSpec(memory_space=VMEM)] * len(outs),
        out_shape=[VMEM(s, d) for s, d in outs],
        scratch_shapes=[s if not isinstance(s, tuple) else VMEM(*s) for s in scratch],
        compiler_params=pltpu.CompilerParams(vmem_limit_bytes=16 * 2**20),
        input_output_aliases=aliases or {},
        cost_estimate=pl.CostEstimate(flops=flops, bytes_accessed=4 * 2**20, transcendentals=0),
        name=name,
    )(*args)


def local(features, short_filter, decay_rate, residue, out_weight):
    rows, _, chans = features.shape
    n_ctx = lax.axis_size("ctx")
    tokens = rows * n_ctx
    run = rows // SUB
    halo = lax.ppermute(features[rows - HALO :], "ctx", [(i, i + 1) for i in range(n_ctx - 1)])
    halo = jnp.transpose(halo, (1, 0, 2))
    x = jnp.transpose(features, (1, 0, 2))
    wide = ((rows, chans), f32)
    states = ((MODES, SUB, chans), f32)
    moved = ((run + BACK) * SUB, chans)
    head = 2 * BACK * SUB
    heads, sig, late, taps, rate = call(
        functools.partial(bulk_kernel, tokens),
        [((2, head, chans), f32), wide, states, (short_filter.shape, f32), (decay_rate.shape, f32)],
        [((2, rows, chans), bf16), ((2, *moved), f32), pltpu.SemaphoreType.DMA((4,))],
        "bulk",
        4 * rows * chans * MODES,
        far=(x, short_filter, decay_rate),
    )
    early, ends, send = call(
        functools.partial(edge_kernel, rows, tokens),
        [((BACK * SUB, chans), f32), states, ((n_ctx, MODES, chans), bf16)],
        [((2, BACK * SUB, chans), f32), ((MODES, SUB, LANES), f32)],
        "edge",
        rows * chans * MODES,
        heads,
        halo,
        taps,
        rate,
        late,
    )
    recv = lax.all_to_all(send, "ctx", 0, 0, tiled=True)
    late_rate, late_residue, _ = lax.optimization_barrier((decay_rate, residue, early))
    coef = late_residue * jnp.sqrt(1.0 / tokens - jnp.expm1(late_rate * (-2.0 / tokens)))
    q, y, lead, turn, ready = call(
        functools.partial(inner_kernel, tokens),
        [wide, wide, states, ((rows, rows), bf16), ((chans, READY), bf16)],
        [((rows, chans), bf16), (moved, f32), wide, pltpu.SemaphoreType.DMA((2,))],
        "inner",
        8 * rows * chans * MODES,
        halo,
        taps,
        rate,
        coef,
        sig,
        early,
        ends,
        far=(x, out_weight),
        aliases={6: 1},
    )

    def stream(width):
        return [((chans, width), bf16), pltpu.SemaphoreType.DMA((max(width // 1024, 1),))]

    gated, first, ahead = call(
        functools.partial(gate_kernel, tokens),
        [((rows, chans), bf16), ((rows, WIDTHS[0]), bf16), ((chans, READY), bf16)],
        [wide, *stream(WIDTHS[0] - READY), pltpu.SemaphoreType.DMA],
        "gate",
        2 * rows * chans * WIDTHS[0],
        recv,
        rate,
        lead,
        y,
        q,
        turn,
        ready,
        far=(out_weight,),
    )
    parts, base = [first], WIDTHS[0]
    for width in WIDTHS[1:]:
        parts += call(
            functools.partial(project_kernel, base),
            [((rows, width), bf16)],
            stream(width - READY),
            "project",
            2 * rows * chans * width,
            gated,
            ahead,
            far=(out_weight,),
        )
        base += width
    return jnp.concatenate([reduce_columns(p, 1, m) for p, m in zip(parts, MEET)], axis=1)


def solution(mesh):
    in_specs = (
        P("ctx", None, "tp"),
        P(None, None, "tp"),
        P(None, "tp"),
        P(None, "tp"),
        P("tp", None),
    )
    out_specs = P(("ctx", "tp"), None)
    return jax.shard_map(local, mesh=mesh, in_specs=in_specs, out_specs=out_specs, check_vma=False)
```
